128 devices in a mesh: row: 16 (over y, x_hi, core), col: 8 (over z, x_lo).
Axes of the slice: x: 4 (x_hi: 2, x_lo: 2; x = x_hi * 2 + x_lo), y: 4, z: 4, core: 2. Of those that a mesh axis runs over, the one named last changes fastest.
Arguments:
- x_act: bfloat16 [4096, 7168], P(('row', 'col')), may hold values from -0.09375 to 0.09375
- grad_out: bfloat16 [4096, 28672], P('col', 'row'), may hold values from -6 to 6
- weight: bfloat16 [7168, 28672], P('col', 'row'), may hold values from -0.078125 to 0.078125
- block_mask: int32 [56, 224], P('col', 'row'), may hold values from 0 to 1, as said below
Outputs:
- grad_in: bfloat16 [4096, 7168], P('row', 'col')
- grad_weight: bfloat16 [7168, 28672], P('col', 'row')
The draws below stay inside these ranges and needn't reach their ends.
Inputs may be any that keep to these rules, and one draw needn't show every extreme that they name: `block_mask`: the tile of 7 x 14 blocks that one device holds has at most 26 live blocks, and some tile has exactly 26; every tile has at least half of 26.
All inputs are finite; a program needn't handle non-finite values.
Results may differ from the reference program's by a relative error of at most 0.011.
Values may be sent and summed in bfloat16 or wider, within the bound.
No kernel may reach another device: no remote copies, remote signals or barrier semaphores. Data moves between devices by JAX's collectives and lax.ppermute only.
A program may use at most 128 MiB of HBM per device.

```python
import jax
import jax.numpy as jnp
from jax import lax

D = 7168
F = 28672
BLK = 128
TOKENS = 4096
DBLK = 7
FBLK = 14
CAP = 26


def draw_block_mask(key, part):
    key = jax.random.fold_in(key, 11)
    key_count, key_top, key_score = jax.random.split(key, 3)
    tiles_d = D // BLK // DBLK
    tiles_f = F // BLK // FBLK
    inner = DBLK * FBLK
    counts = jax.random.randint(key_count, (tiles_d, tiles_f), (CAP + 1) // 2, CAP + 1)
    top = jax.random.randint(key_top, (), 0, tiles_d * tiles_f)
    places = jnp.arange(tiles_d * tiles_f, dtype=jnp.int32).reshape(tiles_d, tiles_f)
    counts = jnp.where(places == top, CAP, counts)
    scores = jax.random.randint(key_score, (tiles_d, tiles_f, inner), 0, 2 ** 20) * inner
    scores = scores + jnp.arange(inner, dtype=jnp.int32)
    ranks = jnp.argsort(jnp.argsort(scores, axis=-1), axis=-1)
    live = (ranks < counts[:, :, None]).astype(jnp.int32)
    live = live.reshape(tiles_d, tiles_f, DBLK, FBLK)
    return jnp.transpose(live, (0, 2, 1, 3)).reshape(D // BLK, F // BLK)


def with_spikes(array, rng, source, target, shards_of, factor):
    def block_of(dim):
        return (jnp.arange(array.shape[dim]) // (array.shape[dim] // shards_of)).reshape((-1,) + (1,) * (array.ndim - 1 - dim))

    first = jax.random.permutation(rng, shards_of)[block_of(target)]
    second = (block_of(target) + shards_of // 2) % shards_of
    return jnp.where((block_of(source) == first) | (block_of(source) == second), factor * array, array)


def block_levels(key, shape, pieces, low, top_value):
    loudness = 1.0
    for dim, parts in pieces:
        draws = jax.random.uniform(jax.random.fold_in(jax.random.fold_in(key, 6), dim), (parts,), jnp.float32, low / len(pieces), top_value / len(pieces))
        loudness = loudness * jnp.repeat(jnp.exp(draws), shape[dim] // parts).reshape((-1,) + (1,) * (len(shape) - 1 - dim))
    return loudness


def centred(stream_key, dims, width, reach, pieces=(), kind=jnp.bfloat16):
    loudness = block_levels(stream_key, dims, pieces, -0.22, 0.18) if pieces else 1.0
    drawn = jax.random.normal(stream_key, dims, jnp.float32) * width * loudness
    return jnp.minimum(jnp.maximum(drawn, -reach), reach).astype(kind)


def gaussian_with(rng, dims, spread, bound, pieces, heavy, held_as=jnp.bfloat16):
    drawn = spread * jax.random.normal(rng, dims, jnp.float32)
    if pieces:
        drawn = drawn * block_levels(rng, dims, pieces, -0.22, 0.18)
    return jnp.clip(with_spikes(drawn, jax.random.fold_in(rng, 3), *heavy), -bound, bound).astype(held_as)


def setup_inputs(seed: int = 0) -> dict:
    streams_of = jax.random.split(jax.random.key(seed), 5)
    return {
        "x_act": centred(streams_of[0], (TOKENS, D), TOKENS ** -0.5, 0.09375, ((0, 128),)),
        "grad_out": gaussian_with(streams_of[1], (TOKENS, F), 1.0, 6.0, ((0, 8), (1, 16)), (1, 0, 16, 2.0)),
        "weight": centred(streams_of[2], (D, F), (F // 5) ** -0.5, 0.078125, ((0, 8), (1, 16))),
        "block_mask": draw_block_mask(jax.random.fold_in(streams_of[4], 71), 0),
    }


def reference(x_act, grad_out, weight, block_mask):
    def one_row(index):
        wrow = lax.dynamic_slice_in_dim(weight, index * BLK, BLK, 0)
        mrow = jnp.repeat(block_mask[index], BLK)
        masked = wrow * mrow.astype(jnp.bfloat16)
        xcol = lax.dynamic_slice_in_dim(x_act, index * BLK, BLK, 1)
        wgrad = jnp.dot(xcol.T, grad_out, preferred_element_type=jnp.float32) * mrow.astype(jnp.float32)
        xgrad = jnp.dot(grad_out, masked.T, preferred_element_type=jnp.float32)
        return wgrad.astype(jnp.bfloat16), xgrad.astype(jnp.bfloat16)

    wgrads, xgrads = lax.map(one_row, jnp.arange(D // BLK, dtype=jnp.int32))
    grad_weight = wgrads.reshape(D, F)
    grad_in = jnp.transpose(xgrads, (1, 0, 2)).reshape(TOKENS, D)
    return grad_in, grad_weight
```

```python
import functools
import itertools

import jax
import jax.numpy as jnp
import numpy as np
from jax import lax
from jax.experimental import pallas as pl
from jax.experimental.pallas import tpu as pltpu
from jax.sharding import Mesh, PartitionSpec as P

AXES = ("y", "xh", "co", "z", "xl")
SIZES = (4, 2, 2, 4, 2)
BLK = 128
CAP = 26
ROWS = 32
PARTS = 2
F32 = jnp.float32
BF16 = jnp.bfloat16
COORDS = list(itertools.product(*(range(n) for n in SIZES)))
VMEM = pl.BlockSpec(memory_space=pltpu.VMEM)
SMEM = pl.BlockSpec(memory_space=pltpu.SMEM)
ANY = pl.BlockSpec(memory_space=pl.ANY)
Y, XH, CO, Z, XL = range(5)


def send(value, target):
    pairs = []
    for at in COORDS:
        to = target(*at)
        if to is not None:
            pairs.append((COORDS.index(at), COORDS.index(to)))
    return lax.ppermute(value, AXES, pairs)


def to_y(step):
    return lambda y, xh, co, z, xl: ((y + step) % 4, xh, co, z, xl)


def to_z(step):
    return lambda y, xh, co, z, xl: (y, xh, co, (z + step) % 4, xl)


def to_core(y, xh, co, z, xl):
    return (y, xh, 1 - co, z, xl)


def to_pair(y, xh, co, z, xl):
    return (y, xh, co, z, 1 - xl)


def along_x(moves):
    def target(y, xh, co, z, xl):
        x = 2 * xh + xl
        if x not in moves:
            return None
        return (y, moves[x] // 2, co, z, moves[x] % 2)

    return target


def out(shape, dtype=BF16):
    return jax.ShapeDtypeStruct(shape, dtype)


def call(kernel, ins, outs, operands, scratch=(), flops=0, limit=28):
    return pl.pallas_call(
        kernel,
        out_shape=tuple(shape for shape, _ in outs),
        in_specs=list(ins),
        out_specs=tuple(spec for _, spec in outs),
        scratch_shapes=list(scratch),
        compiler_params=pltpu.CompilerParams(vmem_limit_bytes=limit * 2 ** 20),
        cost_estimate=pl.CostEstimate(flops=flops, bytes_accessed=max(1024, flops // 200), transcendentals=0),
    )(*operands)


def move(pairs, sems):
    copies = [
        pltpu.make_async_copy(source, target, sems.at[n])
        for n, (source, target) in enumerate(pairs)
    ]
    for copy in copies:
        copy.start()
    return copies


def list_live(mask_ref, list_ref):
    dblk, fblk = mask_ref.shape
    for slot in range(CAP):
        list_ref[slot] = fblk

    def row(i, slot):
        list_ref[ROWS + i] = slot

        def one(j, slot):
            is_live = mask_ref[i, j]

            @pl.when(is_live == 1)
            def _():
                list_ref[slot] = i * 16 + j

            return slot + is_live

        return lax.fori_loop(0, fblk, one, slot)

    list_ref[ROWS + dblk] = lax.fori_loop(0, dblk, row, jnp.int32(0))


def stacked(sources, target):
    pairs, start = [], 0
    for source in sources:
        size = source.shape[0]
        pairs.append((source, target.at[pl.ds(start, size)]))
        start += size
    return pairs


def each_slot(list_ref, body):
    def one(slot, _):
        place = list_ref[slot]
        body(place >> 4, place & 15, slot)
        return 0

    lax.fori_loop(0, CAP, one, 0)


def span(index):
    return pl.ds(pl.multiple_of(index * BLK, BLK), BLK)


def slices_kernel(at_ref, x_ref, x0, x1, x2, x3, sems):
    z, xh = at_ref[Z], at_ref[XH]
    depth = x0.shape[1] // 2
    pairs = []
    for step, x_out in enumerate((x0, x1, x2, x3)):
        there = (z + step) % 4
        for tile, which in enumerate((xh, 1 - xh)):
            start = pl.multiple_of((there * 2 + which) * depth, BLK)
            pairs.append(
                (x_ref.at[:, pl.ds(start, depth)], x_out.at[:, pl.ds(tile * depth, depth)])
            )
    for copy in move(pairs, sems):
        copy.wait()


def compact_kernel(mask_ref, w_ref, out_ref, list_ref, held, sems):
    list_live(mask_ref, list_ref)
    last = mask_ref.shape[1] - 1
    copies = []
    for slot in range(CAP):
        place = list_ref[slot]
        source = w_ref.at[span(place >> 4), span(jnp.minimum(place & 15, last))]
        copies.append(pltpu.make_async_copy(source, held.at[slot], sems.at[slot]))
        copies[slot].start()
    for slot in range(CAP):
        copies[slot].wait()
        out_ref[slot] = held[slot].T


def order_kernel(at_ref, x0, x1, x2, x3, out_ref, sems):
    z = at_ref[Z]
    pairs = [(x_in, out_ref.at[(z + step) % 4]) for step, x_in in enumerate((x0, x1, x2, x3))]
    for copy in move(pairs, sems):
        copy.wait()


def turn_kernel(at_ref, mine, got_a, got_b, out_ref, rows):
    x = at_ref[XH] * 2 + at_ref[XL]
    count = mine.shape[1]

    def put(source, which):
        for n in range(4):
            rows[(2 * n + which) * count : (2 * n + which + 1) * count, :] = source[n]

    for which, near, far in ((0, 0, 1), (1, 3, 2)):
        pl.when(x == near)(functools.partial(put, mine, which))
        pl.when(x == far)(functools.partial(put, got_b, which))
        pl.when((x != near) & (x != far))(functools.partial(put, got_a, which))
    tiles, depth, _ = out_ref.shape
    for tile in range(tiles):
        for i in range(depth // BLK):
            start = tile * depth + i * BLK
            out_ref[tile, i * BLK : (i + 1) * BLK, :] = rows[:, start : start + BLK].T


def partial_kernel(count, at_ref, list_ref, pair_list_ref, blocks_ref, pair_blocks_ref, *refs):
    co = at_ref[CO]
    g_refs, refs = refs[:-9], refs[-9:]
    keep_ref, give_ref, blocks, grows, total, sums, g_sems, w_sems, o_sems = refs
    toks, depth = sums.shape[2], sums.shape[3] // 2
    loads = move(stacked(g_refs, grows), g_sems)
    loads += move([(blocks_ref, blocks.at[0]), (pair_blocks_ref, blocks.at[1])], w_sems)
    for load in loads:
        load.wait()

    def rows_of(place):
        return grows[:, span(place & 15)]

    stores = []
    for tile, slots in enumerate((list_ref, pair_list_ref)):

        def row(i, _):
            first, end = slots[ROWS + i], slots[ROWS + i + 1]
            total[...] = jnp.zeros_like(total)

            def add(slot, size):
                left = [rows_of(slots[slot + n]) for n in range(size)]
                right = blocks[tile, pl.ds(slot, size)].reshape(size * BLK, BLK)
                total[...] += jnp.dot(
                    jnp.concatenate(left, axis=1), right, preferred_element_type=F32
                )

            def four(n, _):
                add(first + 4 * n, 4)
                return 0

            size = end - first
            lax.fori_loop(0, size >> 2, four, 0)
            pl.when((size & 2) == 2)(lambda: add(first + ((size >> 2) << 2), 2))
            pl.when((size & 1) == 1)(lambda: add(end - 1, 1))
            cols = span(i + tile * (depth // BLK))
            for r in range(2 * count):
                rows = total[r * toks : (r + 1) * toks, :].astype(BF16)
                sums[(r % 2) ^ co, r // 2, :, cols] = rows
            return 0

        lax.fori_loop(0, depth // BLK, row, 0)
        half = pl.ds(tile * depth, depth)
        stores += move(
            [
                (sums.at[1, :, :, half], give_ref.at[:, :, half]),
                (sums.at[0, :, :, half], keep_ref.at[:, :, half]),
            ],
            o_sems.at[pl.ds(2 * tile, 2)],
        )
    for store in stores:
        store.wait()


def add_core_kernel(at_ref, near, far, near_got, far_got, *outs):
    toks = outs[0].shape[0]
    half = toks // 2
    chunks = ((near, near_got, 0), (near, near_got, 1), (far, far_got, 0), (near, near_got, 2))

    def cut(turn):
        def total(step, start, size):
            kept, got, n = chunks[(step + turn) % 4]
            rows = pl.ds(start, size)
            return (kept[n, rows, :].astype(F32) + got[n, rows, :].astype(F32)).astype(BF16)

        low, high = outs[-2:]
        for part in range(PARTS):
            base, up, down = outs[3 * part : 3 * part + 3]
            start = part * toks
            base[...] = total(0, start, toks)
            up[...] = total(1, start, toks)
            down[...] = total(3, start, toks)
            low[part] = total(2, start, half)
            high[part] = total(2, start + half, half)

    turned = (at_ref[Y] - at_ref[Z]) & 3
    for turn in range(4):
        pl.when(turned == turn)(functools.partial(cut, turn))


def add_far_kernel(part, up, down, low, high, up_out, down_out):
    half = low.shape[1]
    up_out[:half] = (up[:half].astype(F32) + low[part].astype(F32)).astype(BF16)
    up_out[half:] = up[half:]
    down_out[:half] = down[:half]
    down_out[half:] = (down[half:].astype(F32) + high[part].astype(F32)).astype(BF16)


def add_near_kernel(at_ref, base, up, down, own, to_a, to_b):
    xh, xl = at_ref[XH], at_ref[XL]
    total = base[...].astype(F32) + up[...].astype(F32) + down[...].astype(F32)
    total = total.astype(BF16)
    depth = own.shape[1]
    first, second = total[:, :depth], total[:, depth:]
    own[...] = first

    def put(to_first, to_second):
        to_first[...] = first
        to_second[...] = second

    pl.when(xh == xl)(functools.partial(put, to_b, to_a))
    pl.when(xh != xl)(functools.partial(put, to_a, to_b))


def add_last_kernel(at_ref, own0, a0, b0, own1, a1, b1, out_ref):
    x = at_ref[XH] * 2 + at_ref[XL]
    half = own0.shape[0]

    def put(rows, one, two):
        out_ref[rows, :] = (one[...].astype(F32) + two[...].astype(F32)).astype(BF16)

    for part, (own, a, b) in enumerate(((own0, a0, b0), (own1, a1, b1))):
        rows = pl.ds(part * half, half)
        at_end = (x == 0) | (x == 3)
        pl.when(at_end)(functools.partial(put, rows, a, own))
        pl.when(jnp.logical_not(at_end))(functools.partial(put, rows, a, b))


def weight_kernel(tile, chunks, adds, at_ref, list_ref, *refs):
    y, z, co = at_ref[Y], at_ref[Z], at_ref[CO]
    x_refs, refs = refs[:10], refs[10:]
    g_refs, (out_ref, turned, grows, x_sems, g_sems) = refs[:-5], refs[-5:]
    if adds:
        terms, g_refs = g_refs[-1], g_refs[:-1]
    hidden = grows.shape[1]
    toks = x_refs[0].shape[2]
    g_loads = move(stacked(g_refs, grows), g_sems)
    x_loads = []
    for core, (mine, above, below, *far) in ((co, x_refs[:5]), (1 - co, x_refs[5:])):
        for step, source in enumerate((mine.at[tile], above.at[tile], far[tile], below.at[tile])):
            step = (y + step - z) & 3
            needed, spot = step >= 0, step
            if len(chunks) == 3:
                needed, spot = step != 2, step - (step >> 1)
            elif len(chunks) == 2:
                needed, spot = (step >> 1) == (chunks[0] >> 1), step & 1
            lanes = pl.ds(pl.multiple_of((spot * 2 + core) * toks, BLK), toks)
            load = pltpu.make_async_copy(source, turned.at[:, lanes], x_sems.at[len(x_loads)])
            pl.when(needed)(load.start)
            x_loads.append((needed, load))
    for needed, load in x_loads:
        pl.when(needed)(load.wait)
    for load in g_loads:
        load.wait()
    last = hidden // BLK - 1
    for slot in range(CAP):
        place = list_ref[slot]
        i, j = place >> 4, jnp.minimum(place & 15, last)
        total = jnp.dot(
            turned[span(i), :],
            grows[:, span(j)],
            preferred_element_type=F32,
        )
        if adds:
            total = total + terms[slot]
        out_ref[slot] = total.astype(out_ref.dtype)


def combine_kernel(list_ref, own_ref, got_ref, out_ref):
    out_ref[...] = jnp.zeros_like(out_ref)
    last = out_ref.shape[1] // BLK - 1

    def body(i, j, slot):
        @pl.when(j <= last)
        def _():
            out_ref[span(i), span(j)] = (own_ref[slot] + got_ref[slot].astype(F32)).astype(BF16)

    each_slot(list_ref, body)


def after(value, *others):
    return lax.optimization_barrier((value, others))[0]


def on_device(x_act, grad_out, weight, block_mask):
    place = jnp.stack([lax.axis_index(name) for name in AXES]).astype(jnp.int32)
    depth, hidden = weight.shape
    wide = 2 * depth
    chunk = grad_out.shape[0] // 2
    toks = chunk // PARTS
    few = x_act.shape[0]
    dma = pltpu.SemaphoreType.DMA

    def blocks_of(dtype):
        return (out((CAP, BLK, BLK), dtype), VMEM)

    pair_mask = send(block_mask, to_pair)
    x0, x1, x2, x3 = call(
        slices_kernel, [SMEM, VMEM], [(out((few, wide)), ANY)] * 4,
        (place, x_act), [dma((8,))],
    )
    x_from1 = send(x3, to_z(3))
    x_from2 = send(x2, to_z(2))
    x_from3 = send(x1, to_z(1))

    mine = after(grad_out, x_from1, x_from2, x_from3, pair_mask)
    below = send(mine, to_z(1))
    above = send(mine, to_z(-1))

    (by_z,) = call(
        order_kernel, [SMEM] + [ANY] * 4, [(out((4, few, wide)), ANY)],
        (place, after(x0, pair_mask), x_from1, x_from2, x_from3), [dma((4,))],
    )
    slot_list = (out((ROWS + 8,), jnp.int32), SMEM)
    blocks, slots = call(
        compact_kernel, [SMEM, ANY], [blocks_of(BF16), slot_list],
        (after(block_mask, by_z), weight),
        [pltpu.VMEM((CAP, BLK, BLK), BF16), dma((CAP,))], limit=28,
    )
    pair_blocks = send(blocks, to_pair)
    got_a = send(by_z, along_x({0: 2, 1: 0, 2: 3, 3: 1}))
    got_b = send(by_z, along_x({1: 2, 2: 1}))
    (turned,) = call(
        turn_kernel, [SMEM] + [VMEM] * 3, [(out((2, depth, 8 * few)), VMEM)],
        (place, after(by_z, blocks), got_a, got_b), [pltpu.VMEM((8 * few, wide), BF16)], flops=10 ** 10,
    )
    x_below = send(turned, to_y(1))
    x_above = send(turned, to_y(-1))

    def partials(*grads, flops=0):
        count = sum(grad.shape[0] for grad in grads) // (2 * chunk)
        return call(
            functools.partial(partial_kernel, count), [SMEM] * 3 + [ANY] * (2 + len(grads)),
            [(out((count, chunk, wide)), ANY)] * 2,
            (place, slots, pair_slots, blocks, pair_blocks) + grads,
            [
                pltpu.VMEM((2, CAP, BLK, BLK), BF16),
                pltpu.VMEM((2 * count * chunk, hidden), BF16),
                pltpu.VMEM((2 * count * chunk, BLK), F32),
                pltpu.VMEM((2, count, chunk, wide), BF16),
                dma((len(grads),)), dma((2,)), dma((4,)),
            ],
            flops=flops,
        )

    (pair_slots,) = call(
        list_live, [SMEM], [slot_list], (after(pair_mask, pair_blocks),), flops=5 * 10 ** 9
    )
    far_low, far_high = below[:chunk], above[chunk:]
    far_slices = (far_low, far_high)
    far_low = send(far_low, to_z(1))
    far_high = send(far_high, to_z(-1))
    x_near = tuple(send(value, to_core) for value in (after(turned, pair_slots), x_above, x_below))
    x_low, x_high = after((x_below[0], x_above[1]), far_slices, x_near)
    x_low = send(x_low, to_y(1))
    x_high = send(x_high, to_y(-1))
    near, near_give = partials(
        *after((grad_out, above, below), far_slices, x_near), flops=10 ** 10
    )
    near_got = send(after(near_give, far_low, far_high, x_low, x_high), to_core)
    far, far_give = partials(*after((far_low, far_high), near, x_near))
    far_got = send(far_give, to_core)

    every = (
        (0, (grad_out,)), (1, (above,)), (2, (far_low, far_high)), (3, (below,)),
    )

    def weight_grad(tile, dtype, chunks, terms=(), flops=0, last=()):
        grads = sum((values for chunk_at, values in every if chunk_at in chunks), ())
        (sums,) = call(
            functools.partial(weight_kernel, tile, chunks, bool(terms)),
            [SMEM] * 2 + [ANY] * (10 + len(grads)) + [VMEM] * len(terms), [blocks_of(dtype)],
            (after(place, last), (slots, pair_slots)[tile]) + inputs + grads + terms,
            [
                pltpu.VMEM((depth, 2 * len(chunks) * chunk), BF16),
                pltpu.VMEM((2 * len(chunks) * chunk, hidden), BF16),
                dma((8,)), dma((len(grads),)),
            ],
            flops=flops,
        )
        return sums

    row = (out((toks, wide)), VMEM)
    half_rows = (out((PARTS, toks // 2, wide)), VMEM)
    cuts = call(
        add_core_kernel, [SMEM] + [VMEM] * 4, [row] * 3 * PARTS + [half_rows] * 2,
        (place, near, far, near_got, far_got),
    )
    low, high = send(cuts[-2], to_y(1)), send(cuts[-1], to_y(-1))
    x_far = tuple(send(after(value, far), to_core) for value in (x_low, x_high))
    inputs = (turned, x_above, x_below, x_low, x_high) + x_near + x_far
    pair_sum = weight_grad(1, BF16, (0, 1, 2, 3), (), 2 * 10 ** 10, cuts[0])
    pair_got = send(pair_sum, to_pair)
    ends = []
    last = pair_sum
    for part in range(PARTS):
        base, up, down = cuts[3 * part : 3 * part + 3]
        up, down = call(
            functools.partial(add_far_kernel, part), [VMEM] * 4, [row] * 2,
            after((up, down), last) + (low, high),
        )
        ends.append((base, send(up, to_y(1)), send(down, to_y(-1))))
        last = up
    last = own_sum = weight_grad(0, F32, (0, 1, 2, 3), (), 0, last)
    parts = ()
    for base, up, down in ends:
        mine, to_a, to_b = call(
            add_near_kernel, [SMEM] + [VMEM] * 3, [(out((toks, depth)), VMEM)] * 3,
            (place, after(base, last), up, down),
        )
        got_a = send(to_a, along_x({0: 1, 2: 0, 1: 3, 3: 2}))
        got_b = send(to_b, along_x({2: 1, 1: 2}))
        parts += (mine, got_a, got_b)
        last = (got_a, got_b)

    (grad_weight,) = call(
        combine_kernel, [SMEM, VMEM, VMEM], [(out(weight.shape), VMEM)], (slots, own_sum, pair_got),
        flops=10 ** 10,
    )
    (grad_in,) = call(
        add_last_kernel, [SMEM] + [VMEM] * 6, [(out((chunk, depth)), VMEM)], (place,) + parts
    )
    return grad_in, grad_weight


def solution(mesh):
    fine = Mesh(np.asarray(mesh.devices).reshape(SIZES), AXES)
    rows, cols = AXES[:3], AXES[3:]
    return jax.shard_map(
        on_device,
        mesh=fine,
        in_specs=(P(AXES, None), P(cols, rows), P(cols, rows), P(cols, rows)),
        out_specs=(P(rows, cols), P(cols, rows)),
        check_vma=False,
    )
```

```python
import functools
import itertools

import jax
import jax.numpy as jnp
import numpy as np
from jax import lax
from jax.experimental import pallas as pl
from jax.experimental.pallas import tpu as pltpu
from jax.sharding import Mesh, PartitionSpec as P

AXES = ("y", "xh", "co", "z", "xl")
SIZES = (4, 2, 2, 4, 2)
BLK = 128
CAP = 26
ROWS = 32
PARTS = 2
F32 = jnp.float32
BF16 = jnp.bfloat16
COORDS = list(itertools.product(*(range(n) for n in SIZES)))
VMEM = pl.BlockSpec(memory_space=pltpu.VMEM)
SMEM = pl.BlockSpec(memory_space=pltpu.SMEM)
ANY = pl.BlockSpec(memory_space=pl.ANY)
Y, XH, CO, Z, XL = range(5)


def send(value, target):
    pairs = []
    for at in COORDS:
        to = target(*at)
        if to is not None:
            pairs.append((COORDS.index(at), COORDS.index(to)))
    return lax.ppermute(value, AXES, pairs)


def to_y(step):
    return lambda y, xh, co, z, xl: ((y + step) % 4, xh, co, z, xl)


def to_z(step):
    return lambda y, xh, co, z, xl: (y, xh, co, (z + step) % 4, xl)


def to_core(y, xh, co, z, xl):
    return (y, xh, 1 - co, z, xl)


def to_pair(y, xh, co, z, xl):
    return (y, xh, co, z, 1 - xl)


def along_x(moves):
    def target(y, xh, co, z, xl):
        x = 2 * xh + xl
        if x not in moves:
            return None
        return (y, moves[x] // 2, co, z, moves[x] % 2)

    return target


def out(shape, dtype=BF16):
    return jax.ShapeDtypeStruct(shape, dtype)


def call(kernel, ins, outs, operands, scratch=(), flops=0, limit=28):
    return pl.pallas_call(
        kernel,
        out_shape=tuple(shape for shape, _ in outs),
        in_specs=list(ins),
        out_specs=tuple(spec for _, spec in outs),
        scratch_shapes=list(scratch),
        compiler_params=pltpu.CompilerParams(vmem_limit_bytes=limit * 2 ** 20),
        cost_estimate=pl.CostEstimate(flops=flops, bytes_accessed=max(1024, flops // 200), transcendentals=0),
    )(*operands)


def move(pairs, sems):
    copies = [
        pltpu.make_async_copy(source, target, sems.at[n])
        for n, (source, target) in enumerate(pairs)
    ]
    for copy in copies:
        copy.start()
    return copies


def list_live(mask_ref, list_ref):
    dblk, fblk = mask_ref.shape
    for slot in range(CAP):
        list_ref[slot] = fblk

    def row(i, slot):
        list_ref[ROWS + i] = slot

        def one(j, slot):
            is_live = mask_ref[i, j]

            @pl.when(is_live == 1)
            def _():
                list_ref[slot] = i * 16 + j

            return slot + is_live

        return lax.fori_loop(0, fblk, one, slot)

    list_ref[ROWS + dblk] = lax.fori_loop(0, dblk, row, jnp.int32(0))


def stacked(sources, target):
    pairs, start = [], 0
    for source in sources:
        size = source.shape[0]
        pairs.append((source, target.at[pl.ds(start, size)]))
        start += size
    return pairs


def each_slot(list_ref, body):
    def one(slot, _):
        place = list_ref[slot]
        body(place >> 4, place & 15, slot)
        return 0

    lax.fori_loop(0, CAP, one, 0)


def span(index):
    return pl.ds(pl.multiple_of(index * BLK, BLK), BLK)


def slices_kernel(at_ref, x_ref, x0, x1, x2, x3, sems):
    z, xh = at_ref[Z], at_ref[XH]
    depth = x0.shape[1] // 2
    pairs = []
    for step, x_out in enumerate((x0, x1, x2, x3)):
        there = (z + step) % 4
        for tile, which in enumerate((xh, 1 - xh)):
            start = pl.multiple_of((there * 2 + which) * depth, BLK)
            pairs.append(
                (x_ref.at[:, pl.ds(start, depth)], x_out.at[:, pl.ds(tile * depth, depth)])
            )
    for copy in move(pairs, sems):
        copy.wait()


def compact_kernel(mask_ref, w_ref, out_ref, list_ref, held, sems):
    list_live(mask_ref, list_ref)
    last = mask_ref.shape[1] - 1
    copies = []
    for slot in range(CAP):
        place = list_ref[slot]
        source = w_ref.at[span(place >> 4), span(jnp.minimum(place & 15, last))]
        copies.append(pltpu.make_async_copy(source, held.at[slot], sems.at[slot]))
        copies[slot].start()
    for slot in range(CAP):
        copies[slot].wait()
        out_ref[slot] = held[slot].T


def order_kernel(at_ref, x0, x1, x2, x3, out_ref, sems):
    z = at_ref[Z]
    pairs = [(x_in, out_ref.at[(z + step) % 4]) for step, x_in in enumerate((x0, x1, x2, x3))]
    for copy in move(pairs, sems):
        copy.wait()


def turn_kernel(at_ref, mine, got_a, got_b, out_ref, rows):
    x = at_ref[XH] * 2 + at_ref[XL]
    count = mine.shape[1]

    def put(source, which):
        for n in range(4):
            rows[(2 * n + which) * count : (2 * n + which + 1) * count, :] = source[n]

    for which, near, far in ((0, 0, 1), (1, 3, 2)):
        pl.when(x == near)(functools.partial(put, mine, which))
        pl.when(x == far)(functools.partial(put, got_b, which))
        pl.when((x != near) & (x != far))(functools.partial(put, got_a, which))
    tiles, depth, _ = out_ref.shape
    for tile in range(tiles):
        for i in range(depth // BLK):
            start = tile * depth + i * BLK
            out_ref[tile, i * BLK : (i + 1) * BLK, :] = rows[:, start : start + BLK].T


def partial_kernel(count, at_ref, list_ref, pair_list_ref, blocks_ref, pair_blocks_ref, *refs):
    co = at_ref[CO]
    g_refs, refs = refs[:-7], refs[-7:]
    keep_ref, give_ref, grows, total, sums, g_sems, o_sems = refs
    toks, depth = sums.shape[2], sums.shape[3] // 2
    loads = move(stacked(g_refs, grows), g_sems)
    for load in loads:
        load.wait()

    def rows_of(place):
        return grows[:, span(place & 15)]

    stores = []
    sides = ((list_ref, blocks_ref), (pair_list_ref, pair_blocks_ref))
    for tile, (slots, blocks) in enumerate(sides):

        def row(i, _):
            first, end = slots[ROWS + i], slots[ROWS + i + 1]
            total[...] = jnp.zeros_like(total)

            def add(slot, size):
                left = [rows_of(slots[slot + n]) for n in range(size)]
                right = blocks[pl.ds(slot, size)].reshape(size * BLK, BLK)
                total[...] += jnp.dot(
                    jnp.concatenate(left, axis=1), right, preferred_element_type=F32
                )

            def four(n, _):
                add(first + 4 * n, 4)
                return 0

            size = end - first
            lax.fori_loop(0, size >> 2, four, 0)
            pl.when((size & 2) == 2)(lambda: add(first + ((size >> 2) << 2), 2))
            pl.when((size & 1) == 1)(lambda: add(end - 1, 1))
            cols = span(i + tile * (depth // BLK))
            for r in range(2 * count):
                rows = total[r * toks : (r + 1) * toks, :].astype(BF16)
                sums[(r % 2) ^ co, r // 2, :, cols] = rows
            return 0

        lax.fori_loop(0, depth // BLK, row, 0)
        half = pl.ds(tile * depth, depth)
        stores += move(
            [
                (sums.at[1, :, :, half], give_ref.at[:, :, half]),
                (sums.at[0, :, :, half], keep_ref.at[:, :, half]),
            ],
            o_sems.at[pl.ds(2 * tile, 2)],
        )
    for store in stores:
        store.wait()


def add_core_kernel(at_ref, near, far, near_got, far_got, *outs):
    toks = outs[0].shape[0]
    half = toks // 2
    chunks = ((near, near_got, 0), (near, near_got, 1), (far, far_got, 0), (near, near_got, 2))

    def cut(turn):
        def total(step, start, size):
            kept, got, n = chunks[(step + turn) % 4]
            rows = pl.ds(start, size)
            return (kept[n, rows, :].astype(F32) + got[n, rows, :].astype(F32)).astype(BF16)

        low, high = outs[-2:]
        for part in range(PARTS):
            base, up, down = outs[3 * part : 3 * part + 3]
            start = part * toks
            base[...] = total(0, start, toks)
            up[...] = total(1, start, toks)
            down[...] = total(3, start, toks)
            low[part] = total(2, start, half)
            high[part] = total(2, start + half, half)

    turned = (at_ref[Y] - at_ref[Z]) & 3
    for turn in range(4):
        pl.when(turned == turn)(functools.partial(cut, turn))


def add_far_kernel(part, up, down, low, high, up_out, down_out):
    half = low.shape[1]
    up_out[:half] = (up[:half].astype(F32) + low[part].astype(F32)).astype(BF16)
    up_out[half:] = up[half:]
    down_out[:half] = down[:half]
    down_out[half:] = (down[half:].astype(F32) + high[part].astype(F32)).astype(BF16)


def add_near_kernel(at_ref, base, up, down, own, to_a, to_b):
    xh, xl = at_ref[XH], at_ref[XL]
    total = base[...].astype(F32) + up[...].astype(F32) + down[...].astype(F32)
    total = total.astype(BF16)
    depth = own.shape[1]
    first, second = total[:, :depth], total[:, depth:]
    own[...] = first

    def put(to_first, to_second):
        to_first[...] = first
        to_second[...] = second

    pl.when(xh == xl)(functools.partial(put, to_b, to_a))
    pl.when(xh != xl)(functools.partial(put, to_a, to_b))


def add_last_kernel(at_ref, own0, a0, b0, own1, a1, b1, out_ref):
    x = at_ref[XH] * 2 + at_ref[XL]
    half = own0.shape[0]

    def put(rows, one, two):
        out_ref[rows, :] = (one[...].astype(F32) + two[...].astype(F32)).astype(BF16)

    for part, (own, a, b) in enumerate(((own0, a0, b0), (own1, a1, b1))):
        rows = pl.ds(part * half, half)
        at_end = (x == 0) | (x == 3)
        pl.when(at_end)(functools.partial(put, rows, a, own))
        pl.when(jnp.logical_not(at_end))(functools.partial(put, rows, a, b))


def weight_kernel(tile, chunks, adds, at_ref, list_ref, *refs):
    y, z, co = at_ref[Y], at_ref[Z], at_ref[CO]
    x_refs, refs = refs[:10], refs[10:]
    g_refs, (out_ref, turned, grows, x_sems, g_sems) = refs[:-5], refs[-5:]
    if adds:
        terms, g_refs = g_refs[-1], g_refs[:-1]
    hidden = grows.shape[1]
    toks = x_refs[0].shape[2]
    g_loads = move(stacked(g_refs, grows), g_sems)
    x_loads = []
    for core, (mine, above, below, *far) in ((co, x_refs[:5]), (1 - co, x_refs[5:])):
        for step, source in enumerate((mine.at[tile], above.at[tile], far[tile], below.at[tile])):
            step = (y + step - z) & 3
            needed, spot = step >= 0, step
            if len(chunks) == 3:
                needed, spot = step != 2, step - (step >> 1)
            elif len(chunks) == 2:
                needed, spot = (step >> 1) == (chunks[0] >> 1), step & 1
            lanes = pl.ds(pl.multiple_of((spot * 2 + core) * toks, BLK), toks)
            load = pltpu.make_async_copy(source, turned.at[:, lanes], x_sems.at[len(x_loads)])
            pl.when(needed)(load.start)
            x_loads.append((needed, load))
    for needed, load in x_loads:
        pl.when(needed)(load.wait)
    for load in g_loads:
        load.wait()
    last = hidden // BLK - 1
    for slot in range(CAP):
        place = list_ref[slot]
        i, j = place >> 4, jnp.minimum(place & 15, last)
        total = jnp.dot(
            turned[span(i), :],
            grows[:, span(j)],
            preferred_element_type=F32,
        )
        if adds:
            total = total + terms[slot]
        out_ref[slot] = total.astype(out_ref.dtype)


def combine_kernel(list_ref, own_ref, got_ref, out_ref):
    out_ref[...] = jnp.zeros_like(out_ref)
    last = out_ref.shape[1] // BLK - 1

    def body(i, j, slot):
        @pl.when(j <= last)
        def _():
            out_ref[span(i), span(j)] = (own_ref[slot] + got_ref[slot].astype(F32)).astype(BF16)

    each_slot(list_ref, body)


def after(value, *others):
    return lax.optimization_barrier((value, others))[0]


def on_device(x_act, grad_out, weight, block_mask):
    place = jnp.stack([lax.axis_index(name) for name in AXES]).astype(jnp.int32)
    depth, hidden = weight.shape
    wide = 2 * depth
    chunk = grad_out.shape[0] // 2
    toks = chunk // PARTS
    few = x_act.shape[0]
    dma = pltpu.SemaphoreType.DMA

    def blocks_of(dtype):
        return (out((CAP, BLK, BLK), dtype), VMEM)

    pair_mask = send(block_mask, to_pair)
    x0, x1, x2, x3 = call(
        slices_kernel, [SMEM, VMEM], [(out((few, wide)), ANY)] * 4,
        (place, x_act), [dma((8,))],
    )
    x_from1 = send(x3, to_z(3))
    x_from2 = send(x2, to_z(2))
    x_from3 = send(x1, to_z(1))

    mine = after(grad_out, x_from1, x_from2, x_from3, pair_mask)
    below = send(mine, to_z(1))
    above = send(mine, to_z(-1))

    (by_z,) = call(
        order_kernel, [SMEM] + [ANY] * 4, [(out((4, few, wide)), ANY)],
        (place, after(x0, pair_mask), x_from1, x_from2, x_from3), [dma((4,))],
    )
    slot_list = (out((ROWS + 8,), jnp.int32), SMEM)
    blocks, slots = call(
        compact_kernel, [SMEM, ANY], [blocks_of(BF16), slot_list],
        (after(block_mask, by_z), weight),
        [pltpu.VMEM((CAP, BLK, BLK), BF16), dma((CAP,))], limit=28,
    )
    pair_blocks = send(blocks, to_pair)
    got_a = send(by_z, along_x({0: 2, 1: 0, 2: 3, 3: 1}))
    got_b = send(by_z, along_x({1: 2, 2: 1}))
    (turned,) = call(
        turn_kernel, [SMEM] + [VMEM] * 3, [(out((2, depth, 8 * few)), VMEM)],
        (place, after(by_z, blocks), got_a, got_b), [pltpu.VMEM((8 * few, wide), BF16)], flops=10 ** 10,
    )
    x_below = send(turned, to_y(1))
    x_above = send(turned, to_y(-1))

    def partials(*grads, flops=0):
        count = sum(grad.shape[0] for grad in grads) // (2 * chunk)
        return call(
            functools.partial(partial_kernel, count), [SMEM] * 3 + [VMEM] * 2 + [ANY] * len(grads),
            [(out((count, chunk, wide)), ANY)] * 2,
            (place, slots, pair_slots, blocks, pair_blocks) + grads,
            [
                pltpu.VMEM((2 * count * chunk, hidden), BF16),
                pltpu.VMEM((2 * count * chunk, BLK), F32),
                pltpu.VMEM((2, count, chunk, wide), BF16),
                dma((len(grads),)), dma((4,)),
            ],
            flops=flops,
        )

    (pair_slots,) = call(
        list_live, [SMEM], [slot_list], (after(pair_mask, pair_blocks),), flops=5 * 10 ** 9
    )
    far_low, far_high = below[:chunk], above[chunk:]
    far_slices = (far_low, far_high)
    far_low = send(far_low, to_z(1))
    far_high = send(far_high, to_z(-1))
    x_near = tuple(send(value, to_core) for value in (after(turned, pair_slots), x_above, x_below))
    x_low, x_high = after((x_below[0], x_above[1]), far_slices, x_near)
    x_low = send(x_low, to_y(1))
    x_high = send(x_high, to_y(-1))
    near, near_give = partials(
        *after((grad_out, above, below), far_slices, x_near), flops=10 ** 10
    )
    near_got = send(after(near_give, far_low, far_high, x_low, x_high), to_core)
    far, far_give = partials(*after((far_low, far_high), near, x_near))
    far_got = send(far_give, to_core)

    every = (
        (0, (grad_out,)), (1, (above,)), (2, (far_low, far_high)), (3, (below,)),
    )

    def weight_grad(tile, dtype, chunks, terms=(), flops=0, last=()):
        grads = sum((values for chunk_at, values in every if chunk_at in chunks), ())
        (sums,) = call(
            functools.partial(weight_kernel, tile, chunks, bool(terms)),
            [SMEM] * 2 + [ANY] * (10 + len(grads)) + [VMEM] * len(terms), [blocks_of(dtype)],
            (after(place, last), (slots, pair_slots)[tile]) + inputs + grads + terms,
            [
                pltpu.VMEM((depth, 2 * len(chunks) * chunk), BF16),
                pltpu.VMEM((2 * len(chunks) * chunk, hidden), BF16),
                dma((8,)), dma((len(grads),)),
            ],
            flops=flops,
        )
        return sums

    row = (out((toks, wide)), VMEM)
    half_rows = (out((PARTS, toks // 2, wide)), VMEM)
    cuts = call(
        add_core_kernel, [SMEM] + [VMEM] * 4, [row] * 3 * PARTS + [half_rows] * 2,
        (place, near, far, near_got, far_got),
    )
    low, high = send(cuts[-2], to_y(1)), send(cuts[-1], to_y(-1))
    x_far = tuple(send(after(value, far), to_core) for value in (x_low, x_high))
    inputs = (turned, x_above, x_below, x_low, x_high) + x_near + x_far
    pair_sum = weight_grad(1, BF16, (0, 1, 2, 3), (), 2 * 10 ** 10, cuts[0])
    pair_got = send(pair_sum, to_pair)
    ends = []
    last = pair_sum
    for part in range(PARTS):
        base, up, down = cuts[3 * part : 3 * part + 3]
        up, down = call(
            functools.partial(add_far_kernel, part), [VMEM] * 4, [row] * 2,
            after((up, down), last) + (low, high),
        )
        ends.append((base, send(up, to_y(1)), send(down, to_y(-1))))
        last = up
    last = own_sum = weight_grad(0, F32, (0, 1, 2, 3), (), 0, last)
    parts = ()
    for base, up, down in ends:
        mine, to_a, to_b = call(
            add_near_kernel, [SMEM] + [VMEM] * 3, [(out((toks, depth)), VMEM)] * 3,
            (place, after(base, last), up, down),
        )
        got_a = send(to_a, along_x({0: 1, 2: 0, 1: 3, 3: 2}))
        got_b = send(to_b, along_x({2: 1, 1: 2}))
        parts += (mine, got_a, got_b)
        last = got_a

    (grad_weight,) = call(
        combine_kernel, [SMEM, VMEM, VMEM], [(out(weight.shape), VMEM)], (slots, own_sum, pair_got),
        flops=10 ** 10,
    )
    (grad_in,) = call(
        add_last_kernel, [SMEM] + [VMEM] * 6, [(out((chunk, depth)), VMEM)], (place,) + parts
    )
    return grad_in, grad_weight


def solution(mesh):
    fine = Mesh(np.asarray(mesh.devices).reshape(SIZES), AXES)
    rows, cols = AXES[:3], AXES[3:]
    return jax.shard_map(
        on_device,
        mesh=fine,
        in_specs=(P(AXES, None), P(cols, rows), P(cols, rows), P(cols, rows)),
        out_specs=(P(rows, cols), P(cols, rows)),
        check_vma=False,
    )
```
